32 devices in a mesh: ctx: 8 (over z, x), tp: 4 (over y, core).
Axes of the slice: x: 2, y: 2, z: 4, core: 2. Of those that a mesh axis runs over, the one named last changes fastest.
Arguments:
- projections: bfloat16 [2048, 3, 8192], P('ctx', None, 'tp'), may hold values from -6 to 6
- short_filter: float32 [3, 3, 8192], P(None, None, 'tp'), may hold values from -3 to 3
- decay_rates: float32 [16, 8192], P(None, 'tp'), may hold values from 1.4648437e-05 to 1
- residues: float32 [16, 8192], P(None, 'tp'), may hold values from -2.4 to 2.4
- out_weight: bfloat16 [8192, 4096], P('tp'), may hold values from -0.0625 to 0.0625
Outputs:
- projected: bfloat16 [2048, 4096], P(('ctx', 'tp'))
The draws below stay inside these ranges and needn't reach their ends.
All inputs are finite; a program needn't handle non-finite values.
Results may differ from the reference program's by a relative error of at most 0.005.
Values may be sent and summed in bfloat16 or wider, within the bound.
A program may use at most 320 MiB of HBM per device.

```python
import math
import jax
import jax.numpy as jnp
from jax import lax

D = 8192
DOUT = 4096
MODES = 16
STRETCH = 64
TOKENS = 2048
N_TP = 4


def draw_decay_rates(key, part):
    base = jax.random.fold_in(key, 7001)
    key_slow, key_fast, key_pick = jax.random.split(base, 3)
    fast_share = 0.0625
    fast_low = 0.08
    fast_high = 0.6
    slow_low = math.log(0.03 / TOKENS)
    slow_high = math.log(0.03)
    slow = jnp.exp(jax.random.uniform(key_slow, (MODES, D), jnp.float32, slow_low, slow_high))
    fast = jnp.exp(jax.random.uniform(key_fast, (MODES, D), jnp.float32, math.log(fast_low), math.log(fast_high)))
    picked = jax.random.uniform(key_pick, (MODES, D), jnp.float32) < fast_share
    return jnp.where(picked, fast, slow).astype(jnp.float32)


def block_scale(rng, shape, cuts, smallest, high):
    def one(dim, shards_of):
        draws = jax.random.uniform(jax.random.fold_in(jax.random.fold_in(rng, 6), dim), (shards_of,), jnp.float32, smallest / len(cuts), high / len(cuts))
        return jnp.repeat(jnp.exp(draws), shape[dim] // shards_of).reshape((-1,) + (1,) * (len(shape) - dim - 1))

    factor_of = one(*cuts[0])
    for cut in cuts[1:]:
        factor_of = factor_of * one(*cut)
    return factor_of


def normal_values(key, extent, scale, limit, cuts=(), kind=jnp.bfloat16):
    values = jax.random.normal(key, extent, jnp.float32) * scale
    if len(cuts) > 0:
        values = block_scale(key, extent, cuts, -0.22, 0.18) * values
    return jnp.clip(values, min=-limit, max=limit).astype(kind)


def setup_inputs(seed: int = 0) -> dict:
    streams_of = jax.random.split(jax.random.key(seed), 6)
    projections = normal_values(streams_of[0], (TOKENS, 3, D), 1.0, 6.0, ((0, 8), (2, 4)))
    short_filter = normal_values(streams_of[1], (3, 3, D), 0.6, 3.0, ((2, 4),), jnp.float32)
    decay_rates = draw_decay_rates(jax.random.fold_in(streams_of[5], 71), 0)
    residues = normal_values(streams_of[3], (MODES, D), 0.4, 2.4, ((1, 4),), jnp.float32)
    out_weight = normal_values(streams_of[4], (D, DOUT), D ** -0.5, 0.0625, ((0, 4),))
    return {"projections": projections, "short_filter": short_filter, "decay_rates": decay_rates, "residues": residues, "out_weight": out_weight}


def make_tables(rates, weights_in, block_len):
    scaled = weights_in * jnp.sqrt(2.0 * rates)
    offsets = jnp.arange(block_len).astype(jnp.float32)
    hvalues = lax.optimization_barrier(jnp.sum(scaled[None] * jnp.exp(-rates[None] * offsets[:, None, None]), axis=1))
    spread = (jnp.arange(block_len)[:, None] - jnp.arange(block_len)[None, :]).astype(jnp.int32)
    toeplitz = jnp.where((spread >= 0)[:, :, None], hvalues[jnp.clip(spread, 0, block_len - 1)], 0.0)
    ending = jnp.exp(-rates[None] * (block_len - 1.0 - offsets)[:, None, None])
    entering = scaled[None] * jnp.exp(-rates[None] * (offsets + 1.0)[:, None, None])
    return (toeplitz, ending, entering)

def causal_conv(product, rates, weights_in):
    tok_rows, channels = product.shape
    blocks_count = tok_rows // STRETCH
    toeplitz, ending, entering = make_tables(rates, weights_in, STRETCH)
    pieces = product.reshape(blocks_count, STRETCH, channels)
    hp = lax.Precision.HIGHEST
    inner = jnp.einsum('tsc,ksc->ktc', toeplitz, pieces, precision=hp)
    ends = jnp.einsum('snc,ksc->knc', ending, pieces, precision=hp)
    step_decay = jnp.exp(-rates * STRETCH)

    def advance(state, end_block):
        return (step_decay * state + end_block, state)
    _, states_in = lax.scan(advance, jnp.zeros(rates.shape, jnp.float32), ends)
    outer = jnp.einsum('tnc,knc->ktc', entering, states_in, precision=hp)
    return (inner + outer).reshape(tok_rows, channels)

def reference(projections, short_filter, decay_rates, residues, out_weight):
    group_width = D // N_TP

    def one_group(group_index):
        start = group_index * group_width
        feats = lax.dynamic_slice_in_dim(projections, start, group_width, 2).astype(jnp.float32)
        taps = lax.dynamic_slice_in_dim(short_filter, start, group_width, 2)
        rates = lax.dynamic_slice_in_dim(decay_rates, start, group_width, 1)
        weights_in = lax.dynamic_slice_in_dim(residues, start, group_width, 1)
        padded = jnp.pad(feats, ((2, 0), (0, 0), (0, 0)))
        featured = taps[0] * padded[2:] + taps[1] * padded[1:-1] + taps[2] * padded[:-2]
        product = featured[:, 1, :] * featured[:, 2, :]
        convolved = causal_conv(product, rates, weights_in)
        return (featured[:, 0, :] * convolved).astype(jnp.bfloat16)
    groups = lax.map(one_group, jnp.arange(N_TP, dtype=jnp.int32))
    gated = jnp.transpose(groups, (1, 0, 2)).reshape(TOKENS, D)
    return jnp.dot(gated, out_weight, preferred_element_type=jnp.float32).astype(jnp.bfloat16)
```

```python
import functools

import jax
import jax.numpy as jnp
from jax import lax
from jax.experimental import pallas as pl
from jax.experimental.pallas import tpu as pltpu
from jax.sharding import PartitionSpec as P

LANES = 128
CHUNKS = 8
PAD = 8
GROUPS = 4
WIDTH = 512
UNROLL = 8
MESH = pl.DeviceIdType.MESH
F32 = jnp.float32
BF16 = jnp.bfloat16


def kernel(
    n_ctx, x_hbm, taps_ref, rates_ref, res_ref, w_hbm, out_ref,
    xb, xs, yl, qf, gb, wv, pt, excl, halo_out, halo_in, st_out, st_in,
    decay_all, carry, keep, pair_out, pair_in, far_out, far_in,
    x_sem, w_sem, halo_sem, st_send, st_recv, pair_send, pair_recv, far_send, far_recv,
):
    me = lax.axis_index("ctx")
    tp = lax.axis_index("tp")
    chip, core = tp // 2, tp % 2
    sibling = chip * 2 + (1 - core)
    opposite = (1 - chip) * 2 + core
    toks, channels = xb.shape[1], xb.shape[2]
    step = toks // CHUNKS
    tiles = channels // LANES
    per_group = tiles // GROUPS
    gwidth = channels // GROUPS
    n_out = w_hbm.shape[1] // WIDTH
    share = toks // 4

    x_copy = pltpu.make_async_copy(x_hbm, xb, x_sem)
    x_copy.start()
    w_copy = pltpu.make_async_copy(w_hbm, wv, w_sem)

    barrier = pltpu.get_barrier_semaphore()

    @pl.loop(1, n_ctx)
    def _(k):
        pl.semaphore_signal(
            barrier, inc=1, device_id=(lax.rem(me + k, n_ctx), tp), device_id_type=MESH
        )

    for other in (sibling, opposite):
        pl.semaphore_signal(barrier, inc=1, device_id=(me, other), device_id_type=MESH)

    x_copy.wait()
    w_copy.start()
    for j in range(3):
        tail = xb[j, toks - 16 :, :].astype(F32)
        halo_out[2 * j : 2 * j + 2, :] = tail[14:16]
    halo_out[6:8, :] = jnp.zeros((2, channels), F32)

    pl.semaphore_wait(barrier, n_ctx + 1)

    halo_copy = pltpu.make_async_remote_copy(
        src_ref=halo_out, dst_ref=halo_in, send_sem=halo_sem.at[0], recv_sem=halo_sem.at[1],
        device_id=(lax.rem(me + 1, n_ctx), tp), device_id_type=MESH,
    )

    @pl.when(me < n_ctx - 1)
    def _():
        halo_copy.start()

    @pl.loop(0, tiles)
    def _(c):
        lane = pl.ds(pl.multiple_of(c * LANES, LANES), LANES)
        for j in range(3):
            xs[j, c, PAD:, :] = xb[j, :, lane].astype(F32)

    @pl.when(me == 0)
    def _():
        halo_in[...] = jnp.zeros_like(halo_in)

    @pl.when(me > 0)
    def _():
        halo_copy.wait_recv()

    place = lax.broadcasted_iota(jnp.int32, (1, CHUNKS, LANES), 1)

    def spread(rows):
        return jnp.broadcast_to(rows[:, None, :], (rows.shape[0], CHUNKS, LANES))

    def local_tile(c):
        lane = pl.ds(pl.multiple_of(c * LANES, LANES), LANES)
        rates = rates_ref[:, lane]
        decay = spread(jnp.exp(-rates))
        weight = spread(res_ref[:, lane] * jnp.sqrt(2.0 * rates))
        taps = [[spread(taps_ref[i, j : j + 1, lane])[0] for j in range(3)] for i in range(3)]
        for j in range(3):
            xs[j, c, PAD - 2 : PAD, :] = halo_in[2 * j : 2 * j + 2, lane]

        def at(j, row):
            return xs[j, c, pl.ds(row, CHUNKS, stride=step), :]

        def some(outer, held):
            state, before = held
            before = list(before)
            for k in range(UNROLL):
                i = outer * UNROLL + k
                feats = []
                for j in range(3):
                    now = at(j, PAD + i)
                    one, two = before[2 * j], before[2 * j + 1]
                    feats.append(taps[0][j] * now + taps[1][j] * one + taps[2][j] * two)
                    before[2 * j], before[2 * j + 1] = now, one
                product = feats[1] * feats[2]
                state = decay * state + product[None]
                rows = pl.ds(i, CHUNKS, stride=step)
                yl[c, rows, :] = jnp.sum(weight * state, axis=0)
                qf[c, rows, :] = feats[0]
            return state, tuple(before)

        before = []
        for j in range(3):
            before += [at(j, PAD - 1), at(j, PAD - 2)]
        modes = rates.shape[0]
        zero = jnp.zeros((modes, CHUNKS, LANES), F32)
        state, _ = lax.fori_loop(0, step // UNROLL, some, (zero, tuple(before)))
        for reach in (1, 2, 4):
            fade = spread(jnp.exp(-rates * float(step * reach)))
            moved = pltpu.roll(state, reach, 1)
            state = state + jnp.where(place >= reach, fade * moved, 0.0)
        excl[c] = jnp.where(place >= 1, pltpu.roll(state, 1, 1), 0.0)
        st_out[:, lane] = state[:, CHUNKS - 1, :].astype(BF16)
        decay_all[:, lane] = jnp.exp(-rates * float(toks))

    def state_copy(g, src, dst):
        cols = pl.ds(g * gwidth, gwidth)
        return pltpu.make_async_remote_copy(
            src_ref=st_out.at[:, cols], dst_ref=st_in.at[src, :, cols],
            send_sem=st_send.at[dst, g], recv_sem=st_recv.at[src, g],
            device_id=(dst, tp), device_id_type=MESH,
        )

    for g in range(GROUPS):
        @pl.loop(g * per_group, (g + 1) * per_group)
        def _(c):
            local_tile(c)

        @pl.loop(me + 1, n_ctx)
        def _(dst):
            state_copy(g, me, dst).start()

    def carried_tile(c):
        lane = pl.ds(pl.multiple_of(c * LANES, LANES), LANES)
        rates = rates_ref[:, lane]
        decay = spread(jnp.exp(-rates))
        weight = res_ref[:, lane] * jnp.sqrt(2.0 * rates) * jnp.exp(-rates)
        starts = (place * step).astype(F32)
        into = excl[c] + jnp.exp(-spread(rates) * starts) * spread(carry[:, lane])
        state = spread(weight) * into

        def some(outer, state):
            for k in range(UNROLL):
                rows = pl.ds(outer * UNROLL + k, CHUNKS, stride=step)
                yl[c, rows, :] = qf[c, rows, :] * (yl[c, rows, :] + jnp.sum(state, axis=0))
                state = decay * state
            return state

        lax.fori_loop(0, step // UNROLL, some, state)
        gb[:, lane] = yl[c].astype(BF16)

    for g in range(GROUPS):
        cols = pl.ds(g * gwidth, gwidth)
        carry[:, cols] = jnp.zeros((carry.shape[0], gwidth), F32)

        @pl.loop(0, me)
        def _(src):
            state_copy(g, src, me).wait_recv()
            carry[:, cols] = decay_all[:, cols] * carry[:, cols] + st_in[src, :, cols].astype(F32)

        @pl.loop(g * per_group, (g + 1) * per_group)
        def _(c):
            carried_tile(c)

    w_copy.wait()

    def pair_copy(n):
        return pltpu.make_async_remote_copy(
            src_ref=pair_out.at[n], dst_ref=pair_in.at[n],
            send_sem=pair_send.at[n], recv_sem=pair_recv.at[n],
            device_id=(me, sibling), device_id_type=MESH,
        )

    def far_copy(n):
        return pltpu.make_async_remote_copy(
            src_ref=far_out.at[n], dst_ref=far_in.at[n],
            send_sem=far_send.at[n], recv_sem=far_recv.at[n],
            device_id=(me, opposite), device_id_type=MESH,
        )

    def rows_of(which_chip, which_core):
        at = pl.multiple_of((which_chip * 2 + which_core) * share, share)
        return pl.ds(at, share)

    def forward(n):
        pair_copy(n).wait_recv()
        got = keep[n] + pair_in[n].astype(F32)
        far_out[n] = got[:share].astype(BF16)
        far_copy(n).start()
        keep[n, share:, :] = got[share:]

    @pl.loop(0, n_out)
    def _(n):
        cols = pl.ds(pl.multiple_of(n * WIDTH, WIDTH), WIDTH)
        pt[...] = jnp.dot(gb[...], wv[:, cols], preferred_element_type=F32)
        pair_out[n, :share, :] = pt[rows_of(1 - chip, 1 - core), :].astype(BF16)
        pair_out[n, share:, :] = pt[rows_of(chip, 1 - core), :].astype(BF16)
        pair_copy(n).start()
        keep[n, :share, :] = pt[rows_of(1 - chip, core), :]
        keep[n, share:, :] = pt[rows_of(chip, core), :]

        @pl.when(n > 0)
        def _():
            forward(n - 1)

    forward(n_out - 1)

    @pl.loop(0, n_out)
    def _(n):
        cols = pl.ds(pl.multiple_of(n * WIDTH, WIDTH), WIDTH)
        far_copy(n).wait_recv()
        out_ref[:, cols] = (keep[n, share:, :] + far_in[n].astype(F32)).astype(BF16)

    @pl.loop(0, n_out)
    def _(n):
        pair_copy(n).wait_send()
        far_copy(n).wait_send()

    for g in range(GROUPS):
        @pl.loop(me + 1, n_ctx)
        def _(dst):
            state_copy(g, me, dst).wait_send()

    @pl.when(me < n_ctx - 1)
    def _():
        halo_copy.wait_send()


def per_device(n_ctx, projections, short_filter, decay_rates, residues, out_weight):
    x = jnp.transpose(projections, (1, 0, 2))
    _, toks, channels = x.shape
    modes = decay_rates.shape[0]
    dout = out_weight.shape[1]
    tiles = channels // LANES
    n_out = dout // WIDTH
    share = toks // 4
    dma = pltpu.SemaphoreType.DMA
    vmem = pl.BlockSpec(memory_space=pltpu.VMEM)
    hbm = pl.BlockSpec(memory_space=pl.ANY)
    return pl.pallas_call(
        functools.partial(kernel, n_ctx),
        out_shape=jax.ShapeDtypeStruct((share, dout), BF16),
        in_specs=[hbm, vmem, vmem, vmem, hbm],
        out_specs=vmem,
        scratch_shapes=[
            pltpu.VMEM((3, toks, channels), BF16),
            pltpu.VMEM((3, tiles, PAD + toks, LANES), F32),
            pltpu.VMEM((tiles, toks, LANES), F32),
            pltpu.VMEM((tiles, toks, LANES), F32),
            pltpu.VMEM((toks, channels), BF16),
            pltpu.VMEM((channels, dout), BF16),
            pltpu.VMEM((toks, WIDTH), F32),
            pltpu.VMEM((tiles, modes, CHUNKS, LANES), F32),
            pltpu.VMEM((8, channels), F32),
            pltpu.VMEM((8, channels), F32),
            pltpu.VMEM((modes, channels), BF16),
            pltpu.VMEM((n_ctx, modes, channels), BF16),
            pltpu.VMEM((modes, channels), F32),
            pltpu.VMEM((modes, channels), F32),
            pltpu.VMEM((n_out, 2 * share, WIDTH), F32),
            pltpu.VMEM((n_out, 2 * share, WIDTH), BF16),
            pltpu.VMEM((n_out, 2 * share, WIDTH), BF16),
            pltpu.VMEM((n_out, share, WIDTH), BF16),
            pltpu.VMEM((n_out, share, WIDTH), BF16),
            dma, dma, dma((2,)),
            dma((n_ctx, GROUPS)), dma((n_ctx, GROUPS)),
            dma((n_out,)), dma((n_out,)), dma((n_out,)), dma((n_out,)),
        ],
        compiler_params=pltpu.CompilerParams(
            collective_id=0, has_side_effects=True, vmem_limit_bytes=58 * 2**20
        ),
    )(x, short_filter, decay_rates, residues, out_weight)


def solution(mesh):
    placed = (
        P("ctx", None, "tp"),
        P(None, None, "tp"),
        P(None, "tp"),
        P(None, "tp"),
        P("tp", None),
    )
    return jax.shard_map(
        functools.partial(per_device, mesh.shape["ctx"]),
        mesh=mesh, in_specs=placed, out_specs=P(("ctx", "tp"), None), check_vma=False,
    )
```

```python
import functools

import jax
import jax.numpy as jnp
from jax import lax
from jax.experimental import pallas as pl
from jax.experimental.pallas import tpu as pltpu
from jax.sharding import PartitionSpec as P

LANES = 128
CHUNKS = 8
PAD = 8
GROUPS = 4
WIDTH = 512
UNROLL = 8
MESH = pl.DeviceIdType.MESH
F32 = jnp.float32
BF16 = jnp.bfloat16


def summed(terms):
    while terms.shape[0] % 2 == 0:
        middle = terms.shape[0] // 2
        terms = terms[:middle] + terms[middle:]
    return jnp.sum(terms, axis=0)


def kernel(
    n_ctx, x_hbm, taps_ref, rates_ref, res_ref, w_hbm, out_ref,
    xb, xs, pf, qf, yl, gs, ga, gb, wv, pt, excl, fades, halo_out, halo_in, st_out, twin_in, both_out, st_in,
    own_end, decay_all, carry, first, keep, kept, pair_out, pair_in, own_out, own_in, far_out, far_in,
    x_sem, w_sem, halo_sem, twin_send, twin_recv, st_send, st_recv,
    pair_send, pair_recv, own_send, own_recv, far_send, far_recv,
):
    me = lax.axis_index("ctx")
    tp = lax.axis_index("tp")
    pair, odd = me // 2, me % 2
    twin = pair * 2 + (1 - odd)
    chip, core = tp // 2, tp % 2
    sibling = chip * 2 + (1 - core)
    opposite = (1 - chip) * 2 + core
    toks, channels = xb.shape[1], xb.shape[2]
    half = toks // 2
    step = half // CHUNKS
    tiles = channels // LANES
    per_group = tiles // GROUPS
    gwidth = channels // GROUPS
    n_out = w_hbm.shape[1] // WIDTH
    share = toks // 4
    base_a = pl.multiple_of((1 - chip) * half, half)
    base_b = pl.multiple_of(chip * half, half)

    x_copy = pltpu.make_async_copy(x_hbm, xb, x_sem)
    x_copy.start()
    w_copy = pltpu.make_async_copy(w_hbm, wv, w_sem)

    barrier = pltpu.get_barrier_semaphore()

    @pl.loop(1, n_ctx)
    def _(k):
        pl.semaphore_signal(
            barrier, inc=1, device_id=(lax.rem(me + k, n_ctx), tp), device_id_type=MESH
        )

    for other in (sibling, opposite):
        pl.semaphore_signal(barrier, inc=1, device_id=(me, other), device_id_type=MESH)

    x_copy.wait()
    w_copy.start()
    for j in range(3):
        tail = xb[j, toks - 16 :, :].astype(F32)
        halo_out[2 * j : 2 * j + 2, :] = tail[14:16]
    halo_out[6:8, :] = jnp.zeros((2, channels), F32)

    pl.semaphore_wait(barrier, n_ctx + 1)

    halo_copy = pltpu.make_async_remote_copy(
        src_ref=halo_out, dst_ref=halo_in, send_sem=halo_sem.at[0], recv_sem=halo_sem.at[1],
        device_id=(lax.rem(me + 1, n_ctx), tp), device_id_type=MESH,
    )

    @pl.when(me < n_ctx - 1)
    def _():
        halo_copy.start()

    def features(c, lane, rows):
        feats = []
        for j in range(3):
            total = taps_ref[0, j : j + 1, lane] * xs[j, c, PAD : PAD + rows, :]
            for i in (1, 2):
                total += taps_ref[i, j : j + 1, lane] * xs[j, c, PAD - i : PAD - i + rows, :]
            feats.append(total)
        qf[c, :rows, :] = feats[0]
        pf[c, :rows, :] = feats[1] * feats[2]

    @pl.loop(0, tiles)
    def _(c):
        lane = pl.ds(pl.multiple_of(c * LANES, LANES), LANES)
        for j in range(3):
            xs[j, c, :PAD, :] = jnp.zeros((PAD, LANES), F32)
            xs[j, c, PAD:, :] = xb[j, :, lane].astype(F32)
        features(c, lane, toks)

    @pl.when(me == 0)
    def _():
        halo_in[...] = jnp.zeros_like(halo_in)

    @pl.when(me > 0)
    def _():
        halo_copy.wait_recv()

    place = lax.broadcasted_iota(jnp.int32, (1, CHUNKS, LANES), 1)

    def spread(rows):
        return jnp.broadcast_to(rows[:, None, :], (rows.shape[0], CHUNKS, LANES))

    def scanned(state, rates):
        for reach in (1, 2, 4):
            fade = spread(jnp.exp(-rates * float(step * reach)))
            moved = pltpu.roll(state, reach, 1)
            state = state + jnp.where(place >= reach, fade * moved, 0.0)
        return jnp.where(place >= 1, pltpu.roll(state, 1, 1), 0.0), state[:, CHUNKS - 1, :]

    def local_tile(c):
        lane = pl.ds(pl.multiple_of(c * LANES, LANES), LANES)
        rates = rates_ref[:, lane]
        decay = spread(jnp.exp(-rates))
        weight = spread(res_ref[:, lane] * jnp.sqrt(2.0 * rates))
        for j in range(3):
            xs[j, c, PAD - 2 : PAD, :] = halo_in[2 * j : 2 * j + 2, lane]
        features(c, lane, 8)
        zero = jnp.zeros((rates.shape[0], CHUNKS, LANES), F32)

        def ends(outer, state):
            for k in range(UNROLL):
                rows = pl.ds(base_b + outer * UNROLL + k, CHUNKS, stride=step)
                state = decay * state + pf[c, rows, :][None]
            return state

        before_b, total_b = scanned(lax.fori_loop(0, step // UNROLL, ends, zero), rates)
        excl[1, c] = before_b

        def both(outer, state):
            for k in range(UNROLL):
                rows = pl.ds(base_a + outer * UNROLL + k, CHUNKS, stride=step)
                state = decay * state + pf[c, rows, :][None]
                yl[c, pl.ds(outer * UNROLL + k, CHUNKS, stride=step), :] = summed(weight * state)
            return state

        before_a, total_a = scanned(lax.fori_loop(0, step // UNROLL, both, zero), rates)
        excl[0, c] = before_a
        fade = jnp.exp(-rates * float(half))
        early = jnp.where(chip == 0, total_b, total_a)
        late = jnp.where(chip == 0, total_a, total_b)
        first[:, lane] = early
        end = fade * early + late
        own_end[:, lane] = end
        st_out[:, lane] = end.astype(BF16)
        decay_all[:, lane] = jnp.exp(-rates * float(toks))

    def group(g):
        return pl.ds(g * gwidth, gwidth)

    def twin_copy(g):
        return pltpu.make_async_remote_copy(
            src_ref=st_out.at[:, group(g)], dst_ref=twin_in.at[:, group(g)],
            send_sem=twin_send.at[g], recv_sem=twin_recv.at[g],
            device_id=(twin, tp), device_id_type=MESH,
        )

    def state_copy(g, src, dst):
        return pltpu.make_async_remote_copy(
            src_ref=both_out.at[:, group(g)], dst_ref=st_in.at[src, :, group(g)],
            send_sem=st_send.at[dst, g], recv_sem=st_recv.at[src, g],
            device_id=(dst * 2 + odd, tp), device_id_type=MESH,
        )

    def send_both(g):
        cols = group(g)
        twin_copy(g).wait_recv()
        other = twin_in[:, cols].astype(F32)
        own = own_end[:, cols]
        fade = decay_all[:, cols]
        total = jnp.where(odd == 1, fade * other + own, fade * own + other)
        both_out[:, cols] = total.astype(BF16)

        @pl.loop(pair + 1, n_ctx // 2)
        def _(dst):
            state_copy(g, pair, dst).start()

    for g in range(GROUPS):
        @pl.loop(g * per_group, (g + 1) * per_group)
        def _(c):
            local_tile(c)

        twin_copy(g).start()
        if g > 0:
            send_both(g - 1)
    send_both(GROUPS - 1)

    def steady(c):
        lane = pl.ds(pl.multiple_of(c * LANES, LANES), LANES)
        rates = rates_ref[:, lane]
        weight = spread(res_ref[:, lane] * jnp.sqrt(2.0 * rates) * jnp.exp(-rates))
        starts = (place * step).astype(F32)
        fade = weight * jnp.exp(-spread(rates) * starts)
        base = weight * excl[0, c]
        fades[c] = fade
        excl[0, c] = base + jnp.where(chip == 0, fade * spread(first[:, lane]), 0.0)

    @pl.loop(0, tiles)
    def _(c):
        steady(c)

    def entering(c, lane, rates):
        starts = (place * step).astype(F32)
        into = carry[:, lane]
        late = jnp.exp(-rates * float(half)) * into + first[:, lane]
        into = jnp.where(chip == 1, late, into)
        return excl[1, c] + jnp.exp(-spread(rates) * starts) * spread(into)

    def carried_tile(c):
        lane = pl.ds(pl.multiple_of(c * LANES, LANES), LANES)
        rates = rates_ref[:, lane]
        decay = spread(jnp.exp(-rates))
        into = carry[:, lane]
        into = jnp.where(chip == 0, jnp.exp(-rates * float(half)) * into, into)
        state = excl[0, c] + fades[c] * spread(into)

        def some(outer, state):
            for k in range(UNROLL):
                i = outer * UNROLL + k
                local = pl.ds(i, CHUNKS, stride=step)
                gate = qf[c, pl.ds(base_a + i, CHUNKS, stride=step), :]
                gs[local, :] = gate * (yl[c, local, :] + summed(state))
                state = decay * state
            return state

        lax.fori_loop(0, step // UNROLL, some, state)
        ga[:, lane] = gs[...].astype(BF16)

    def own_tile(c):
        lane = pl.ds(pl.multiple_of(c * LANES, LANES), LANES)
        rates = rates_ref[:, lane]
        decay = spread(jnp.exp(-rates))
        weight = spread(res_ref[:, lane] * jnp.sqrt(2.0 * rates))
        state = entering(c, lane, rates)

        def some(outer, state):
            for k in range(UNROLL):
                i = outer * UNROLL + k
                rows = pl.ds(base_b + i, CHUNKS, stride=step)
                state = decay * state + pf[c, rows, :][None]
                gs[pl.ds(i, CHUNKS, stride=step), :] = qf[c, rows, :] * summed(weight * state)
            return state

        lax.fori_loop(0, step // UNROLL, some, state)
        gb[:, lane] = gs[...].astype(BF16)

    for g in range(GROUPS):
        cols = group(g)
        carry[:, cols] = jnp.zeros((carry.shape[0], gwidth), F32)

        @pl.loop(0, pair)
        def _(src):
            fade = decay_all[:, cols] * decay_all[:, cols]
            state_copy(g, src, pair).wait_recv()
            carry[:, cols] = fade * carry[:, cols] + st_in[src, :, cols].astype(F32)

        @pl.when(odd == 1)
        def _():
            carry[:, cols] = decay_all[:, cols] * carry[:, cols] + twin_in[:, cols].astype(F32)

        @pl.loop(g * per_group, (g + 1) * per_group)
        def _(c):
            carried_tile(c)

    w_copy.wait()

    def to_sibling(n, out, into, send, recv):
        return pltpu.make_async_remote_copy(
            src_ref=out.at[n], dst_ref=into.at[n], send_sem=send.at[n], recv_sem=recv.at[n],
            device_id=(me, sibling), device_id_type=MESH,
        )

    def pair_copy(n):
        return to_sibling(n, pair_out, pair_in, pair_send, pair_recv)

    def own_copy(n):
        return to_sibling(n, own_out, own_in, own_send, own_recv)

    def far_copy(n):
        return pltpu.make_async_remote_copy(
            src_ref=far_out.at[n], dst_ref=far_in.at[n],
            send_sem=far_send.at[n], recv_sem=far_recv.at[n],
            device_id=(me, opposite), device_id_type=MESH,
        )

    mine = pl.ds(pl.multiple_of(core * share, share), share)
    theirs = pl.ds(pl.multiple_of((1 - core) * share, share), share)

    def forward(n):
        pair_copy(n).wait_recv()
        far_out[n] = (keep[n] + pair_in[n].astype(F32)).astype(BF16)
        far_copy(n).start()

    def columns(n):
        return pl.ds(pl.multiple_of(n * WIDTH, WIDTH), WIDTH)

    @pl.loop(0, n_out)
    def _(n):
        pt[...] = jnp.dot(ga[...], wv[:, columns(n)], preferred_element_type=F32)
        pair_out[n] = pt[theirs, :].astype(BF16)
        pair_copy(n).start()
        keep[n] = pt[mine, :]

        @pl.when(n > 0)
        def _():
            forward(n - 1)

    forward(n_out - 1)

    @pl.loop(0, tiles)
    def _(c):
        own_tile(c)

    @pl.loop(0, n_out)
    def _(n):
        pt[...] = jnp.dot(gb[...], wv[:, columns(n)], preferred_element_type=F32)
        own_out[n] = pt[theirs, :].astype(BF16)
        own_copy(n).start()
        kept[n] = pt[mine, :]

    @pl.loop(0, n_out)
    def _(n):
        own_copy(n).wait_recv()
        far_copy(n).wait_recv()
        total = kept[n] + own_in[n].astype(F32) + far_in[n].astype(F32)
        out_ref[:, columns(n)] = total.astype(BF16)

    @pl.loop(0, n_out)
    def _(n):
        pair_copy(n).wait_send()
        own_copy(n).wait_send()
        far_copy(n).wait_send()

    for g in range(GROUPS):
        twin_copy(g).wait_send()

        @pl.loop(pair + 1, n_ctx // 2)
        def _(dst):
            state_copy(g, pair, dst).wait_send()

    @pl.when(me < n_ctx - 1)
    def _():
        halo_copy.wait_send()


def per_device(n_ctx, projections, short_filter, decay_rates, residues, out_weight):
    x = jnp.transpose(projections, (1, 0, 2))
    _, toks, channels = x.shape
    modes = decay_rates.shape[0]
    dout = out_weight.shape[1]
    tiles = channels // LANES
    n_out = dout // WIDTH
    share = toks // 4
    dma = pltpu.SemaphoreType.DMA
    vmem = pl.BlockSpec(memory_space=pltpu.VMEM)
    hbm = pl.BlockSpec(memory_space=pl.ANY)
    return pl.pallas_call(
        functools.partial(kernel, n_ctx),
        out_shape=jax.ShapeDtypeStruct((share, dout), BF16),
        in_specs=[hbm, vmem, vmem, vmem, hbm],
        out_specs=vmem,
        scratch_shapes=[
            pltpu.VMEM((3, toks, channels), BF16),
            pltpu.VMEM((3, tiles, PAD + toks, LANES), F32),
            pltpu.VMEM((tiles, toks, LANES), F32),
            pltpu.VMEM((tiles, toks, LANES), F32),
            pltpu.VMEM((tiles, toks // 2, LANES), F32),
            pltpu.VMEM((toks // 2, LANES), F32),
            pltpu.VMEM((toks // 2, channels), BF16),
            pltpu.VMEM((toks // 2, channels), BF16),
            pltpu.VMEM((channels, dout), BF16),
            pltpu.VMEM((toks // 2, WIDTH), F32),
            pltpu.VMEM((2, tiles, modes, CHUNKS, LANES), F32),
            pltpu.VMEM((tiles, modes, CHUNKS, LANES), F32),
            pltpu.VMEM((8, channels), F32),
            pltpu.VMEM((8, channels), F32),
            pltpu.VMEM((modes, channels), BF16),
            pltpu.VMEM((modes, channels), BF16),
            pltpu.VMEM((modes, channels), BF16),
            pltpu.VMEM((n_ctx // 2, modes, channels), BF16),
            pltpu.VMEM((modes, channels), F32),
            pltpu.VMEM((modes, channels), F32),
            pltpu.VMEM((modes, channels), F32),
            pltpu.VMEM((modes, channels), F32),
            pltpu.VMEM((n_out, share, WIDTH), F32),
            pltpu.VMEM((n_out, share, WIDTH), F32),
            pltpu.VMEM((n_out, share, WIDTH), BF16),
            pltpu.VMEM((n_out, share, WIDTH), BF16),
            pltpu.VMEM((n_out, share, WIDTH), BF16),
            pltpu.VMEM((n_out, share, WIDTH), BF16),
            pltpu.VMEM((n_out, share, WIDTH), BF16),
            pltpu.VMEM((n_out, share, WIDTH), BF16),
            dma, dma, dma((2,)),
            dma((GROUPS,)), dma((GROUPS,)),
            dma((n_ctx // 2, GROUPS)), dma((n_ctx // 2, GROUPS)),
            dma((n_out,)), dma((n_out,)), dma((n_out,)), dma((n_out,)),
            dma((n_out,)), dma((n_out,)),
        ],
        compiler_params=pltpu.CompilerParams(
            collective_id=0, has_side_effects=True, vmem_limit_bytes=58 * 2**20
        ),
    )(x, short_filter, decay_rates, residues, out_weight)


def solution(mesh):
    placed = (
        P("ctx", None, "tp"),
        P(None, None, "tp"),
        P(None, "tp"),
        P(None, "tp"),
        P("tp", None),
    )
    return jax.shard_map(
        functools.partial(per_device, mesh.shape["ctx"]),
        mesh=mesh, in_specs=placed, out_specs=P(("ctx", "tp"), None), check_vma=False,
    )
```

```python
import functools

import jax
import jax.numpy as jnp
from jax import lax
from jax.experimental import pallas as pl
from jax.experimental.pallas import tpu as pltpu
from jax.sharding import PartitionSpec as P

LANES = 128
CHUNKS = 8
PAD = 8
GROUPS = 4
WIDTH = 512
UNROLL = 8
MESH = pl.DeviceIdType.MESH
F32 = jnp.float32
BF16 = jnp.bfloat16


def summed(terms):
    while terms.shape[0] % 2 == 0:
        middle = terms.shape[0] // 2
        terms = terms[:middle] + terms[middle:]
    return jnp.sum(terms, axis=0)


def kernel(
    n_ctx, x_hbm, taps_ref, rates_ref, res_ref, w_hbm, out_ref,
    xb, xs, pf, qf, yl, gs, ga, gb, wv, pt, excl, fades, halo_out, halo_in, st_out, twin_in, both_out, st_in,
    own_end, decay_all, carry, first, keep, kept, pair_out, pair_in, own_out, own_in, far_out, far_in,
    x_sem, w_sem, halo_sem, twin_send, twin_recv, st_send, st_recv,
    pair_send, pair_recv, own_send, own_recv, far_send, far_recv,
):
    me = lax.axis_index("ctx")
    tp = lax.axis_index("tp")
    pair, odd = me // 2, me % 2
    twin = pair * 2 + (1 - odd)
    chip, core = tp // 2, tp % 2
    sibling = chip * 2 + (1 - core)
    opposite = (1 - chip) * 2 + core
    toks, channels = xb.shape[1], xb.shape[2]
    half = toks // 2
    step = half // CHUNKS
    apart = step + 1
    tiles = channels // LANES
    per_group = tiles // GROUPS
    gwidth = channels // GROUPS
    n_out = w_hbm.shape[1] // WIDTH
    share = toks // 4
    base_a = (1 - chip) * (CHUNKS * apart)
    base_b = chip * (CHUNKS * apart)

    x_copy = pltpu.make_async_copy(x_hbm, xb, x_sem)
    x_copy.start()
    w_copy = pltpu.make_async_copy(w_hbm, wv, w_sem)

    barrier = pltpu.get_barrier_semaphore()

    @pl.loop(1, n_ctx)
    def _(k):
        pl.semaphore_signal(
            barrier, inc=1, device_id=(lax.rem(me + k, n_ctx), tp), device_id_type=MESH
        )

    for other in (sibling, opposite):
        pl.semaphore_signal(barrier, inc=1, device_id=(me, other), device_id_type=MESH)

    x_copy.wait()
    w_copy.start()
    for j in range(3):
        tail = xb[j, toks - 16 :, :].astype(F32)
        halo_out[2 * j : 2 * j + 2, :] = tail[14:16]
    halo_out[6:8, :] = jnp.zeros((2, channels), F32)

    pl.semaphore_wait(barrier, n_ctx + 1)

    halo_copy = pltpu.make_async_remote_copy(
        src_ref=halo_out, dst_ref=halo_in, send_sem=halo_sem.at[0], recv_sem=halo_sem.at[1],
        device_id=(lax.rem(me + 1, n_ctx), tp), device_id_type=MESH,
    )

    @pl.when(me < n_ctx - 1)
    def _():
        halo_copy.start()

    def features(c, lane, rows):
        feats = []
        for j in range(3):
            total = taps_ref[0, j : j + 1, lane] * xs[j, c, PAD : PAD + rows, :]
            for i in (1, 2):
                total += taps_ref[i, j : j + 1, lane] * xs[j, c, PAD - i : PAD - i + rows, :]
            feats.append(total)
        product = feats[1] * feats[2]
        for low in range(0, rows, step):
            high = min(low + step, rows)
            at = low // step * apart
            qf[c, at : at + high - low, :] = feats[0][low:high]
            pf[c, at : at + high - low, :] = product[low:high]

    @pl.loop(0, tiles)
    def _(c):
        lane = pl.ds(pl.multiple_of(c * LANES, LANES), LANES)
        for j in range(3):
            xs[j, c, :PAD, :] = jnp.zeros((PAD, LANES), F32)
            xs[j, c, PAD:, :] = xb[j, :, lane].astype(F32)
        features(c, lane, toks)

    @pl.when(me == 0)
    def _():
        halo_in[...] = jnp.zeros_like(halo_in)

    @pl.when(me > 0)
    def _():
        halo_copy.wait_recv()

    place = lax.broadcasted_iota(jnp.int32, (1, CHUNKS, LANES), 1)

    def spread(rows):
        return jnp.broadcast_to(rows[:, None, :], (rows.shape[0], CHUNKS, LANES))

    def scanned(state, rates):
        for reach in (1, 2, 4):
            fade = spread(jnp.exp(-rates * float(step * reach)))
            moved = pltpu.roll(state, reach, 1)
            state = state + jnp.where(place >= reach, fade * moved, 0.0)
        return jnp.where(place >= 1, pltpu.roll(state, 1, 1), 0.0), state[:, CHUNKS - 1, :]

    def local_tile(c):
        lane = pl.ds(pl.multiple_of(c * LANES, LANES), LANES)
        rates = rates_ref[:, lane]
        decay = spread(jnp.exp(-rates))
        weight = spread(res_ref[:, lane] * jnp.sqrt(2.0 * rates))
        for j in range(3):
            xs[j, c, PAD - 2 : PAD, :] = halo_in[2 * j : 2 * j + 2, lane]
        features(c, lane, 8)
        zero = jnp.zeros((rates.shape[0], CHUNKS, LANES), F32)

        def ends(outer, state):
            for k in range(UNROLL):
                rows = pl.ds(base_b + outer * UNROLL + k, CHUNKS, stride=apart)
                state = decay * state + pf[c, rows, :][None]
            return state

        before_b, total_b = scanned(lax.fori_loop(0, step // UNROLL, ends, zero), rates)
        excl[1, c] = before_b

        def both(outer, state):
            for k in range(UNROLL):
                rows = pl.ds(base_a + outer * UNROLL + k, CHUNKS, stride=apart)
                state = decay * state + pf[c, rows, :][None]
                yl[c, pl.ds(outer * UNROLL + k, CHUNKS, stride=apart), :] = summed(weight * state)
            return state

        before_a, total_a = scanned(lax.fori_loop(0, step // UNROLL, both, zero), rates)
        excl[0, c] = before_a
        fade = jnp.exp(-rates * float(half))
        early = jnp.where(chip == 0, total_b, total_a)
        late = jnp.where(chip == 0, total_a, total_b)
        first[:, lane] = early
        end = fade * early + late
        own_end[:, lane] = end
        st_out[:, lane] = end.astype(BF16)
        decay_all[:, lane] = jnp.exp(-rates * float(toks))

    def group(g):
        return pl.ds(g * gwidth, gwidth)

    def twin_copy(g):
        return pltpu.make_async_remote_copy(
            src_ref=st_out.at[:, group(g)], dst_ref=twin_in.at[:, group(g)],
            send_sem=twin_send.at[g], recv_sem=twin_recv.at[g],
            device_id=(twin, tp), device_id_type=MESH,
        )

    def state_copy(g, src, dst):
        return pltpu.make_async_remote_copy(
            src_ref=both_out.at[:, group(g)], dst_ref=st_in.at[src, :, group(g)],
            send_sem=st_send.at[dst, g], recv_sem=st_recv.at[src, g],
            device_id=(dst * 2 + odd, tp), device_id_type=MESH,
        )

    def send_both(g):
        cols = group(g)
        twin_copy(g).wait_recv()
        other = twin_in[:, cols].astype(F32)
        own = own_end[:, cols]
        fade = decay_all[:, cols]
        total = jnp.where(odd == 1, fade * other + own, fade * own + other)
        both_out[:, cols] = total.astype(BF16)

        @pl.loop(pair + 1, n_ctx // 2)
        def _(dst):
            state_copy(g, pair, dst).start()

    for g in range(GROUPS):
        @pl.loop(g * per_group, (g + 1) * per_group)
        def _(c):
            local_tile(c)

        twin_copy(g).start()
        if g > 0:
            send_both(g - 1)
    send_both(GROUPS - 1)

    def steady(c):
        lane = pl.ds(pl.multiple_of(c * LANES, LANES), LANES)
        rates = rates_ref[:, lane]
        weight = spread(res_ref[:, lane] * jnp.sqrt(2.0 * rates) * jnp.exp(-rates))
        starts = (place * step).astype(F32)
        fade = weight * jnp.exp(-spread(rates) * starts)
        base = weight * excl[0, c]
        fades[c] = fade
        excl[0, c] = base + jnp.where(chip == 0, fade * spread(first[:, lane]), 0.0)

    @pl.loop(0, tiles)
    def _(c):
        steady(c)

    def entering(c, lane, rates):
        starts = (place * step).astype(F32)
        into = carry[:, lane]
        late = jnp.exp(-rates * float(half)) * into + first[:, lane]
        into = jnp.where(chip == 1, late, into)
        return excl[1, c] + jnp.exp(-spread(rates) * starts) * spread(into)

    def carried_tile(c):
        lane = pl.ds(pl.multiple_of(c * LANES, LANES), LANES)
        rates = rates_ref[:, lane]
        decay = spread(jnp.exp(-rates))
        into = carry[:, lane]
        into = jnp.where(chip == 0, jnp.exp(-rates * float(half)) * into, into)
        state = excl[0, c] + fades[c] * spread(into)

        def some(outer, state):
            for k in range(UNROLL):
                i = outer * UNROLL + k
                local = pl.ds(i, CHUNKS, stride=apart)
                gate = qf[c, pl.ds(base_a + i, CHUNKS, stride=apart), :]
                gs[local, :] = gate * (yl[c, local, :] + summed(state))
                state = decay * state
            return state

        lax.fori_loop(0, step // UNROLL, some, state)
        for s in range(CHUNKS):
            ga[s * step : (s + 1) * step, lane] = gs[s * apart : s * apart + step, :].astype(BF16)

    def own_tile(c):
        lane = pl.ds(pl.multiple_of(c * LANES, LANES), LANES)
        rates = rates_ref[:, lane]
        decay = spread(jnp.exp(-rates))
        weight = spread(res_ref[:, lane] * jnp.sqrt(2.0 * rates))
        state = entering(c, lane, rates)

        def some(outer, state):
            for k in range(UNROLL):
                i = outer * UNROLL + k
                rows = pl.ds(base_b + i, CHUNKS, stride=apart)
                state = decay * state + pf[c, rows, :][None]
                gs[pl.ds(i, CHUNKS, stride=apart), :] = qf[c, rows, :] * summed(weight * state)
            return state

        lax.fori_loop(0, step // UNROLL, some, state)
        for s in range(CHUNKS):
            gb[s * step : (s + 1) * step, lane] = gs[s * apart : s * apart + step, :].astype(BF16)

    for g in range(GROUPS):
        cols = group(g)
        carry[:, cols] = jnp.zeros((carry.shape[0], gwidth), F32)

        @pl.loop(0, pair)
        def _(src):
            fade = decay_all[:, cols] * decay_all[:, cols]
            state_copy(g, src, pair).wait_recv()
            carry[:, cols] = fade * carry[:, cols] + st_in[src, :, cols].astype(F32)

        @pl.when(odd == 1)
        def _():
            carry[:, cols] = decay_all[:, cols] * carry[:, cols] + twin_in[:, cols].astype(F32)

        @pl.loop(g * per_group, (g + 1) * per_group)
        def _(c):
            carried_tile(c)

    w_copy.wait()

    def to_sibling(n, out, into, send, recv):
        return pltpu.make_async_remote_copy(
            src_ref=out.at[n], dst_ref=into.at[n], send_sem=send.at[n], recv_sem=recv.at[n],
            device_id=(me, sibling), device_id_type=MESH,
        )

    def pair_copy(n):
        return to_sibling(n, pair_out, pair_in, pair_send, pair_recv)

    def own_copy(n):
        return to_sibling(n, own_out, own_in, own_send, own_recv)

    def far_copy(n):
        return pltpu.make_async_remote_copy(
            src_ref=far_out.at[n], dst_ref=far_in.at[n],
            send_sem=far_send.at[n], recv_sem=far_recv.at[n],
            device_id=(me, opposite), device_id_type=MESH,
        )

    mine = pl.ds(pl.multiple_of(core * share, share), share)
    theirs = pl.ds(pl.multiple_of((1 - core) * share, share), share)

    def forward(n):
        pair_copy(n).wait_recv()
        far_out[n] = (keep[n] + pair_in[n].astype(F32)).astype(BF16)
        far_copy(n).start()

    def columns(n):
        return pl.ds(pl.multiple_of(n * WIDTH, WIDTH), WIDTH)

    @pl.loop(0, n_out)
    def _(n):
        pt[...] = jnp.dot(ga[...], wv[:, columns(n)], preferred_element_type=F32)
        pair_out[n] = pt[theirs, :].astype(BF16)
        pair_copy(n).start()
        keep[n] = pt[mine, :]

        @pl.when(n > 0)
        def _():
            forward(n - 1)

    forward(n_out - 1)

    @pl.loop(0, tiles)
    def _(c):
        own_tile(c)

    @pl.loop(0, n_out)
    def _(n):
        pt[...] = jnp.dot(gb[...], wv[:, columns(n)], preferred_element_type=F32)
        own_out[n] = pt[theirs, :].astype(BF16)
        own_copy(n).start()
        kept[n] = pt[mine, :]

    @pl.loop(0, n_out)
    def _(n):
        own_copy(n).wait_recv()
        far_copy(n).wait_recv()
        total = kept[n] + own_in[n].astype(F32) + far_in[n].astype(F32)
        out_ref[:, columns(n)] = total.astype(BF16)

    @pl.loop(0, n_out)
    def _(n):
        pair_copy(n).wait_send()
        own_copy(n).wait_send()
        far_copy(n).wait_send()

    for g in range(GROUPS):
        twin_copy(g).wait_send()

        @pl.loop(pair + 1, n_ctx // 2)
        def _(dst):
            state_copy(g, pair, dst).wait_send()

    @pl.when(me < n_ctx - 1)
    def _():
        halo_copy.wait_send()


def per_device(n_ctx, projections, short_filter, decay_rates, residues, out_weight):
    x = jnp.transpose(projections, (1, 0, 2))
    _, toks, channels = x.shape
    modes = decay_rates.shape[0]
    dout = out_weight.shape[1]
    tiles = channels // LANES
    n_out = dout // WIDTH
    share = toks // 4
    padded = toks // 2 + CHUNKS
    dma = pltpu.SemaphoreType.DMA
    vmem = pl.BlockSpec(memory_space=pltpu.VMEM)
    hbm = pl.BlockSpec(memory_space=pl.ANY)
    return pl.pallas_call(
        functools.partial(kernel, n_ctx),
        out_shape=jax.ShapeDtypeStruct((share, dout), BF16),
        in_specs=[hbm, vmem, vmem, vmem, hbm],
        out_specs=vmem,
        scratch_shapes=[
            pltpu.VMEM((3, toks, channels), BF16),
            pltpu.VMEM((3, tiles, PAD + toks, LANES), F32),
            pltpu.VMEM((tiles, 2 * padded, LANES), F32),
            pltpu.VMEM((tiles, 2 * padded, LANES), F32),
            pltpu.VMEM((tiles, padded, LANES), F32),
            pltpu.VMEM((padded, LANES), F32),
            pltpu.VMEM((toks // 2, channels), BF16),
            pltpu.VMEM((toks // 2, channels), BF16),
            pltpu.VMEM((channels, dout), BF16),
            pltpu.VMEM((toks // 2, WIDTH), F32),
            pltpu.VMEM((2, tiles, modes, CHUNKS, LANES), F32),
            pltpu.VMEM((tiles, modes, CHUNKS, LANES), F32),
            pltpu.VMEM((8, channels), F32),
            pltpu.VMEM((8, channels), F32),
            pltpu.VMEM((modes, channels), BF16),
            pltpu.VMEM((modes, channels), BF16),
            pltpu.VMEM((modes, channels), BF16),
            pltpu.VMEM((n_ctx // 2, modes, channels), BF16),
            pltpu.VMEM((modes, channels), F32),
            pltpu.VMEM((modes, channels), F32),
            pltpu.VMEM((modes, channels), F32),
            pltpu.VMEM((modes, channels), F32),
            pltpu.VMEM((n_out, share, WIDTH), F32),
            pltpu.VMEM((n_out, share, WIDTH), F32),
            pltpu.VMEM((n_out, share, WIDTH), BF16),
            pltpu.VMEM((n_out, share, WIDTH), BF16),
            pltpu.VMEM((n_out, share, WIDTH), BF16),
            pltpu.VMEM((n_out, share, WIDTH), BF16),
            pltpu.VMEM((n_out, share, WIDTH), BF16),
            pltpu.VMEM((n_out, share, WIDTH), BF16),
            dma, dma, dma((2,)),
            dma((GROUPS,)), dma((GROUPS,)),
            dma((n_ctx // 2, GROUPS)), dma((n_ctx // 2, GROUPS)),
            dma((n_out,)), dma((n_out,)), dma((n_out,)), dma((n_out,)),
            dma((n_out,)), dma((n_out,)),
        ],
        compiler_params=pltpu.CompilerParams(
            collective_id=0, has_side_effects=True, vmem_limit_bytes=58 * 2**20
        ),
    )(x, short_filter, decay_rates, residues, out_weight)


def solution(mesh):
    placed = (
        P("ctx", None, "tp"),
        P(None, None, "tp"),
        P(None, "tp"),
        P(None, "tp"),
        P("tp", None),
    )
    return jax.shard_map(
        functools.partial(per_device, mesh.shape["ctx"]),
        mesh=mesh, in_specs=placed, out_specs=P(("ctx", "tp"), None), check_vma=False,
    )
```
